32 devices in a mesh: row: 4 (over x, core), col: 4 (over z), layer: 2 (over y).
Axes of the slice: x: 2, y: 2, z: 4, core: 2. Of those that a mesh axis runs over, the one named last changes fastest.
Arguments:
- amplitudes: float32 [1536, 16384], P(('row', 'col', 'layer')), may hold values from -6 to 6
- integrals: float32 [16384, 2048], P(('col', 'layer')), may hold values from -0.046875 to 0.046875
- pair_list: int32 [1536, 2], P(('row', 'col', 'layer')), may hold values from 0 to 199, as said below
- occupied_energy: float32 [200], replicated, may hold values from -1.5 to -0.3
- virtual_energy: float32 [2048], replicated, may hold values from 1 to 4
Outputs:
- ladder_update: float32 [1536, 2048], P(('row', 'col', 'layer'))
The draws below stay inside these ranges and needn't reach their ends.
Inputs may be any that keep to these rules, and one draw needn't show every extreme that they name: `pair_list`: each row (i, j) holds two occupied orbital numbers with i <= j.
All inputs are finite; a program needn't handle non-finite values.
Results may differ from the reference program's by a relative error of at most 0.000071.
Values sent between devices are 32-bit elements; how exact they have to be, the bound alone decides.
A program may use at most 128 MiB of HBM per device.

```python
import jax
import jax.numpy as jnp
from jax import lax

NOCC = 200
K_EF = 16384
N_AB = 2048
PAIRS = 1536


def draw_pair_list(key, part):
    own_key = jax.random.fold_in(key, 7)
    key_one, key_two = jax.random.split(own_key)
    draw_one = jax.random.randint(key_one, (PAIRS,), 0, NOCC, dtype=jnp.int32)
    draw_two = jax.random.randint(key_two, (PAIRS,), 0, NOCC, dtype=jnp.int32)
    lower = jnp.minimum(draw_one, draw_two)
    upper = jnp.maximum(draw_one, draw_two)
    row_index = jnp.arange(PAIRS, dtype=jnp.int32)
    lower = jnp.where(row_index == 0, 0, lower)
    upper = jnp.where(row_index == 0, NOCC - 1, upper)
    return jnp.stack([lower, upper], axis=1).astype(jnp.int32)


def shard_levels(key, extent, cuts, low, high):
    def one(dim, shards_of):
        draws = jax.random.uniform(jax.random.fold_in(jax.random.fold_in(key, 6), dim), (shards_of,), jnp.float32, low / len(cuts), high / len(cuts))
        return jnp.repeat(jnp.exp(draws), extent[dim] // shards_of).reshape((-1,) + (1,) * (len(extent) - dim - 1))

    gain = one(*cuts[0])
    for cut in cuts[1:]:
        gain = gain * one(*cut)
    return gain


def bell_draw(stream_key, shape, scale, bound, pieces=(), kind=jnp.bfloat16):
    gain = shard_levels(stream_key, shape, pieces, -0.22, 0.18) if pieces else 1.0
    values = jax.random.normal(stream_key, shape, jnp.float32) * scale * gain
    return jnp.minimum(jnp.maximum(values, -bound), bound).astype(kind)


def setup_inputs(seed: int = 0) -> dict:
    key_list = jax.random.split(jax.random.key(seed), 6)
    return {
        "amplitudes": bell_draw(key_list[0], (PAIRS, K_EF), 1.0, 6.0, ((0, 32),), jnp.float32),
        "integrals": bell_draw(key_list[1], (K_EF, N_AB), K_EF ** -0.5, 0.046875, ((0, 8),), jnp.float32),
        "pair_list": draw_pair_list(jax.random.fold_in(key_list[5], 71), 0),
        "occupied_energy": jnp.clip(jax.random.uniform(key_list[3], (NOCC,), jnp.float32, -1.5, -0.3), -1.5, -0.3),
        "virtual_energy": jnp.clip(jax.random.uniform(key_list[4], (N_AB,), jnp.float32, 1.0, 4.0), 1.0, 4.0),
    }


def reference(amplitudes, integrals, pair_list, occupied_energy, virtual_energy):
    ladder = jnp.dot(amplitudes, integrals, precision=lax.Precision.HIGHEST, preferred_element_type=jnp.float32)
    occ_first = occupied_energy[pair_list[:, 0]]
    occ_second = occupied_energy[pair_list[:, 1]]
    denominator = virtual_energy[None, :] - occ_first[:, None] - occ_second[:, None]
    return ladder / denominator
```

```python
import functools

import jax
import jax.numpy as jnp
from jax import lax
from jax.experimental import pallas as pl
from jax.experimental.pallas import tpu as pltpu
from jax.sharding import PartitionSpec as P

MESH = pl.DeviceIdType.MESH
CHUNKS = (24, 16, 8)
TILE = 512
AHEAD = 1


def reverse_bits(value, bits):
    out = 0
    for bit in range(bits):
        out |= ((value >> bit) & 1) << (bits - 1 - bit)
    return out


def peer_id(me, k, layers):
    other = jnp.bitwise_xor(me, k)
    return {"col": other // layers, "layer": lax.rem(other, layers)}


def kernel(
    group, layers, chunks, amp, ints, out, got, part, back, high, low, amp_high, amp_low, stage,
    stage_sem, own_sem, amp_send, amp_recv, back_send, back_recv,
):
    bits = group.bit_length() - 1
    depth = ints.shape[0]
    columns = ints.shape[1]
    tiles = columns // TILE
    me = lax.axis_index("col") * layers + lax.axis_index("layer")

    barrier = pltpu.get_barrier_semaphore()
    for k in range(1, group):
        pl.semaphore_signal(barrier, inc=1, device_id=peer_id(me, k, layers), device_id_type=MESH)

    def load_tile(t, slot):
        cols = pl.ds(pl.multiple_of(t * TILE, TILE), TILE)
        return pltpu.make_async_copy(ints.at[:, cols], stage.at[slot], stage_sem.at[slot])

    load_tile(0, 0).start()

    starts = [sum(chunks[:c]) for c in range(len(chunks))]

    def ef_columns(k):
        return pl.ds(pl.multiple_of(jnp.bitwise_xor(me, k) * depth, depth), depth)

    def amp_copy(c, k):
        slot = reverse_bits(k, bits)
        rows = pl.ds(starts[c], chunks[c])
        return pltpu.make_async_remote_copy(
            src_ref=amp.at[rows, ef_columns(k)],
            dst_ref=got.at[slot, rows, :],
            send_sem=amp_send.at[c, slot],
            recv_sem=amp_recv.at[c, slot],
            device_id=peer_id(me, k, layers),
            device_id_type=MESH,
        )

    def send_amp(c):
        for k in reversed(range(1, group)):
            amp_copy(c, k).start()

    own = pltpu.make_async_copy(amp.at[:, ef_columns(0)], got.at[0], own_sem)

    pl.semaphore_wait(barrier, group - 1)
    for c in range(min(AHEAD, len(chunks))):
        send_amp(c)
    own.start()

    @pl.loop(0, tiles)
    def _(t):
        slot = lax.rem(t, 2)

        @pl.when(t + 1 < tiles)
        def _():
            load_tile(t + 1, 1 - slot).start()

        load_tile(t, slot).wait()
        cols = pl.ds(pl.multiple_of(t * TILE, TILE), TILE)
        step = min(depth, 256)

        @pl.loop(0, depth // step)
        def _(i):
            rows = pl.ds(pl.multiple_of(i * step, step), step)
            value = stage[slot, rows, :]
            top = value.astype(jnp.bfloat16)
            high[rows, cols] = top
            low[rows, cols] = (value - top.astype(jnp.float32)).astype(jnp.bfloat16)

    own.wait()

    def back_copy(c, s, t):
        half = group >> (s + 1)
        rows = pl.ds(starts[c], chunks[c])
        cols = pl.ds(pl.multiple_of(t * TILE, TILE), TILE)
        return pltpu.make_async_remote_copy(
            src_ref=part.at[pl.ds(half, half), rows, cols],
            dst_ref=back.at[pl.ds(group - 2 * half, half), rows, cols],
            send_sem=back_send.at[c, s, t],
            recv_sem=back_recv.at[c, s, t],
            device_id=peer_id(me, 1 << s, layers),
            device_id_type=MESH,
        )

    def add_back(c, s, t):
        half = group >> (s + 1)
        rows = pl.ds(starts[c], chunks[c])
        cols = pl.ds(pl.multiple_of(t * TILE, TILE), TILE)
        back_copy(c, s, t).wait_recv()
        if s == bits - 1:
            out[rows, cols] = part[0, rows, cols] + back[group - 2, rows, cols]
            return
        kept = pl.ds(0, half)
        part[kept, rows, cols] += back[pl.ds(group - 2 * half, half), rows, cols]
        back_copy(c, s + 1, t).start()

    def compute(c):
        count = group * chunks[c]
        rows = pl.ds(starts[c], chunks[c])

        @pl.loop(0, tiles)
        def _(t):
            cols = pl.ds(pl.multiple_of(t * TILE, TILE), TILE)
            both = jnp.dot(amp_high[pl.ds(0, count), :], high[:, cols], preferred_element_type=jnp.float32)
            both += jnp.dot(amp_high[pl.ds(0, count), :], low[:, cols], preferred_element_type=jnp.float32)
            both += jnp.dot(amp_low[pl.ds(0, count), :], high[:, cols], preferred_element_type=jnp.float32)
            part[:, rows, cols] = both.reshape(group, chunks[c], TILE)
            back_copy(c, 0, t).start()

    last = len(chunks) - 1
    for c in range(len(chunks)):
        for k in reversed(range(1, group)):
            amp_copy(c, k).wait_recv()
        if c + AHEAD <= last:
            send_amp(c + AHEAD)
        rows = pl.ds(starts[c], chunks[c])
        value = got[:, rows, :].reshape(group * chunks[c], depth)
        top = value.astype(jnp.bfloat16)
        amp_high[pl.ds(0, group * chunks[c]), :] = top
        amp_low[pl.ds(0, group * chunks[c]), :] = (value - top.astype(jnp.float32)).astype(jnp.bfloat16)
        compute(c)
        if c > 0:
            for t in range(tiles):
                add_back(c - 1, bits - 1, t)
        stop = bits if c == last else bits - 1
        for i in range(tiles + stop - 1):
            for s in range(stop):
                if 0 <= i - s < tiles:
                    add_back(c, s, i - s)

    for c in range(len(chunks)):
        for k in range(1, group):
            amp_copy(c, k).wait_send()
        for s in range(bits):
            for t in range(tiles):
                back_copy(c, s, t).wait_send()


def energy_lookup(pair_list, occupied_energy):
    occ_index = jnp.arange(occupied_energy.shape[0], dtype=jnp.int32)
    occ_first = jnp.sum(
        jnp.where(pair_list[:, 0:1] == occ_index[None, :], occupied_energy[None, :], 0.0), axis=1
    )
    occ_second = jnp.sum(
        jnp.where(pair_list[:, 1:2] == occ_index[None, :], occupied_energy[None, :], 0.0), axis=1
    )
    return (occ_first, occ_second)


def body(group, layers, amplitudes, integrals, pair_list, occupied_energy, virtual_energy):
    count = amplitudes.shape[0]
    depth, columns = integrals.shape
    bits = group.bit_length() - 1
    tiles = columns // TILE
    chunks = CHUNKS
    most = group * max(chunks)
    n = len(chunks)
    ladder = pl.pallas_call(
        functools.partial(kernel, group, layers, chunks),
        out_shape=jax.ShapeDtypeStruct((count, columns), jnp.float32),
        in_specs=[pl.BlockSpec(memory_space=pl.ANY)] * 2,
        out_specs=pl.BlockSpec(memory_space=pltpu.VMEM),
        scratch_shapes=[
            pltpu.VMEM((group, count, depth), jnp.float32),
            pltpu.VMEM((group, count, columns), jnp.float32),
            pltpu.VMEM((group - 1, count, columns), jnp.float32),
            pltpu.VMEM((depth, columns), jnp.bfloat16),
            pltpu.VMEM((depth, columns), jnp.bfloat16),
            pltpu.VMEM((most, depth), jnp.bfloat16),
            pltpu.VMEM((most, depth), jnp.bfloat16),
            pltpu.VMEM((2, depth, TILE), jnp.float32),
            pltpu.SemaphoreType.DMA((2,)),
            pltpu.SemaphoreType.DMA,
            pltpu.SemaphoreType.DMA((n, group)),
            pltpu.SemaphoreType.DMA((n, group)),
            pltpu.SemaphoreType.DMA((n, bits, tiles)),
            pltpu.SemaphoreType.DMA((n, bits, tiles)),
        ],
        compiler_params=pltpu.CompilerParams(
            collective_id=0, has_side_effects=True, vmem_limit_bytes=63 * 1024 * 1024
        ),
        cost_estimate=pl.CostEstimate(
            flops=6 * group * count * depth * columns, bytes_accessed=4 * (count * group * depth + depth * columns),
            transcendentals=0,
        ),
    )(amplitudes, integrals)
    occ_first, occ_second = energy_lookup(pair_list, occupied_energy)
    denominator = virtual_energy[None, :] - occ_first[:, None] - occ_second[:, None]
    return ladder / denominator


def solution(mesh):
    in_specs = (
        P(("row", "col", "layer"), None),
        P(("col", "layer"), None),
        P(("row", "col", "layer"), None),
        P(),
        P(),
    )
    out_specs = P(("row", "col", "layer"), None)
    layers = mesh.shape["layer"]
    group = mesh.shape["col"] * layers
    return jax.shard_map(
        functools.partial(body, group, layers), mesh=mesh, in_specs=in_specs, out_specs=out_specs, check_vma=False
    )
```

```python
import functools

import jax
import jax.numpy as jnp
from jax import lax
from jax.experimental import pallas as pl
from jax.experimental.pallas import tpu as pltpu
from jax.sharding import PartitionSpec as P

MESH = pl.DeviceIdType.MESH
CHUNKS = (16, 16, 16)
TILE = 512
RETURN = 1024
LAST = 512
AHEAD = 2


def reverse_bits(value, bits):
    out = 0
    for bit in range(bits):
        out |= ((value >> bit) & 1) << (bits - 1 - bit)
    return out


def peer_id(me, k, layers):
    other = jnp.bitwise_xor(me, k)
    return {"col": other // layers, "layer": lax.rem(other, layers)}


def kernel(
    group, layers, chunks, amp, ints, out, got, part, back, high, low, amp_high, amp_low, stage,
    stage_sem, own_sem, amp_send, amp_recv, back_send, back_recv,
):
    bits = group.bit_length() - 1
    depth = ints.shape[0]
    columns = ints.shape[1]
    tiles = columns // TILE
    me = lax.axis_index("col") * layers + lax.axis_index("layer")

    barrier = pltpu.get_barrier_semaphore()
    for k in range(1, group):
        pl.semaphore_signal(barrier, inc=1, device_id=peer_id(me, k, layers), device_id_type=MESH)

    def load_tile(t, slot):
        cols = pl.ds(pl.multiple_of(t * TILE, TILE), TILE)
        return pltpu.make_async_copy(ints.at[:, cols], stage.at[slot], stage_sem.at[slot])

    load_tile(0, 0).start()

    starts = [sum(chunks[:c]) for c in range(len(chunks))]

    def ef_columns(k):
        return pl.ds(pl.multiple_of(jnp.bitwise_xor(me, k) * depth, depth), depth)

    def amp_copy(c, k):
        slot = reverse_bits(k, bits)
        rows = pl.ds(starts[c], chunks[c])
        return pltpu.make_async_remote_copy(
            src_ref=amp.at[rows, ef_columns(k)],
            dst_ref=got.at[slot, rows, :],
            send_sem=amp_send.at[c, slot],
            recv_sem=amp_recv.at[c, slot],
            device_id=peer_id(me, k, layers),
            device_id_type=MESH,
        )

    def send_amp(c):
        for k in reversed(range(1, group)):
            amp_copy(c, k).start()

    own = pltpu.make_async_copy(amp.at[:, ef_columns(0)], got.at[0], own_sem)

    pl.semaphore_wait(barrier, group - 1)
    for c in range(min(AHEAD, len(chunks))):
        send_amp(c)
    own.start()

    @pl.loop(0, tiles)
    def _(t):
        slot = lax.rem(t, 2)

        @pl.when(t + 1 < tiles)
        def _():
            load_tile(t + 1, 1 - slot).start()

        load_tile(t, slot).wait()
        cols = pl.ds(pl.multiple_of(t * TILE, TILE), TILE)
        step = min(depth, 256)

        @pl.loop(0, depth // step)
        def _(i):
            rows = pl.ds(pl.multiple_of(i * step, step), step)
            value = stage[slot, rows, :]
            top = value.astype(jnp.bfloat16)
            high[rows, cols] = top
            low[rows, cols] = (value - top.astype(jnp.float32)).astype(jnp.bfloat16)

    own.wait()

    last = len(chunks) - 1

    def width(c):
        return LAST if c == last else RETURN

    def tiles_of(c):
        return columns // width(c)

    def tile_columns(c, t):
        return pl.ds(pl.multiple_of(t * width(c), width(c)), width(c))

    def back_copy(c, s, t):
        half = group >> (s + 1)
        rows = pl.ds(starts[c], chunks[c])
        cols = tile_columns(c, t)
        return pltpu.make_async_remote_copy(
            src_ref=part.at[pl.ds(half, half), rows, cols],
            dst_ref=back.at[pl.ds(group - 2 * half, half), rows, cols],
            send_sem=back_send.at[c, s, t],
            recv_sem=back_recv.at[c, s, t],
            device_id=peer_id(me, 1 << s, layers),
            device_id_type=MESH,
        )

    def add_back(c, s, t):
        half = group >> (s + 1)
        rows = pl.ds(starts[c], chunks[c])
        cols = tile_columns(c, t)
        back_copy(c, s, t).wait_recv()
        if s == bits - 1:
            out[rows, cols] = part[0, rows, cols] + back[group - 2, rows, cols]
            return
        kept = pl.ds(0, half)
        part[kept, rows, cols] += back[pl.ds(group - 2 * half, half), rows, cols]
        back_copy(c, s + 1, t).start()

    def add_all(c, s):
        for t in range(tiles_of(c)):
            add_back(c, s, t)

    def compute(c):
        count = group * chunks[c]
        rows = pl.ds(starts[c], chunks[c])
        value = got[:, rows, :].reshape(count, depth)
        top = value.astype(jnp.bfloat16)
        amp_high[pl.ds(0, count), :] = top
        amp_low[pl.ds(0, count), :] = (value - top.astype(jnp.float32)).astype(jnp.bfloat16)

        @pl.loop(0, tiles_of(c))
        def _(t):
            cols = tile_columns(c, t)
            both = jnp.dot(amp_high[pl.ds(0, count), :], high[:, cols], preferred_element_type=jnp.float32)
            both += jnp.dot(amp_high[pl.ds(0, count), :], low[:, cols], preferred_element_type=jnp.float32)
            both += jnp.dot(amp_low[pl.ds(0, count), :], high[:, cols], preferred_element_type=jnp.float32)
            part[:, rows, cols] = both.reshape(group, chunks[c], width(c))
            back_copy(c, 0, t).start()

    for c in range(len(chunks)):
        for k in reversed(range(1, group)):
            amp_copy(c, k).wait_recv()
        if c + AHEAD <= last:
            send_amp(c + AHEAD)
        compute(c)
        for s in range(1, bits):
            if c - s >= 0:
                add_all(c - s, s)
        if c < last:
            add_all(c, 0)

    left = [(c, s) for c in range(last) for s in range(last - c + 1, bits)]
    for c, s in left:
        if s < bits - 1:
            add_all(c, s)
    for i in range(tiles_of(last) + bits - 1):
        for s in range(bits):
            if 0 <= i - s < tiles_of(last):
                add_back(last, s, i - s)
    for c, s in left:
        if s == bits - 1:
            add_all(c, s)

    for c in range(len(chunks)):
        for k in range(1, group):
            amp_copy(c, k).wait_send()
        for s in range(bits):
            for t in range(tiles_of(c)):
                back_copy(c, s, t).wait_send()


def energy_lookup(pair_list, occupied_energy):
    occ_index = jnp.arange(occupied_energy.shape[0], dtype=jnp.int32)
    occ_first = jnp.sum(
        jnp.where(pair_list[:, 0:1] == occ_index[None, :], occupied_energy[None, :], 0.0), axis=1
    )
    occ_second = jnp.sum(
        jnp.where(pair_list[:, 1:2] == occ_index[None, :], occupied_energy[None, :], 0.0), axis=1
    )
    return (occ_first, occ_second)


def body(group, layers, amplitudes, integrals, pair_list, occupied_energy, virtual_energy):
    count = amplitudes.shape[0]
    depth, columns = integrals.shape
    bits = group.bit_length() - 1
    tiles = columns // min(RETURN, LAST)
    chunks = CHUNKS
    most = group * max(chunks)
    n = len(chunks)
    ladder = pl.pallas_call(
        functools.partial(kernel, group, layers, chunks),
        out_shape=jax.ShapeDtypeStruct((count, columns), jnp.float32),
        in_specs=[pl.BlockSpec(memory_space=pl.ANY)] * 2,
        out_specs=pl.BlockSpec(memory_space=pltpu.VMEM),
        scratch_shapes=[
            pltpu.VMEM((group, count, depth), jnp.float32),
            pltpu.VMEM((group, count, columns), jnp.float32),
            pltpu.VMEM((group - 1, count, columns), jnp.float32),
            pltpu.VMEM((depth, columns), jnp.bfloat16),
            pltpu.VMEM((depth, columns), jnp.bfloat16),
            pltpu.VMEM((most, depth), jnp.bfloat16),
            pltpu.VMEM((most, depth), jnp.bfloat16),
            pltpu.VMEM((2, depth, TILE), jnp.float32),
            pltpu.SemaphoreType.DMA((2,)),
            pltpu.SemaphoreType.DMA,
            pltpu.SemaphoreType.DMA((n, group)),
            pltpu.SemaphoreType.DMA((n, group)),
            pltpu.SemaphoreType.DMA((n, bits, tiles)),
            pltpu.SemaphoreType.DMA((n, bits, tiles)),
        ],
        compiler_params=pltpu.CompilerParams(
            collective_id=0, has_side_effects=True, vmem_limit_bytes=63 * 1024 * 1024
        ),
        cost_estimate=pl.CostEstimate(
            flops=6 * group * count * depth * columns, bytes_accessed=4 * (count * group * depth + depth * columns),
            transcendentals=0,
        ),
    )(amplitudes, integrals)
    occ_first, occ_second = energy_lookup(pair_list, occupied_energy)
    denominator = virtual_energy[None, :] - occ_first[:, None] - occ_second[:, None]
    return ladder / denominator


def solution(mesh):
    in_specs = (
        P(("row", "col", "layer"), None),
        P(("col", "layer"), None),
        P(("row", "col", "layer"), None),
        P(),
        P(),
    )
    out_specs = P(("row", "col", "layer"), None)
    layers = mesh.shape["layer"]
    group = mesh.shape["col"] * layers
    return jax.shard_map(
        functools.partial(body, group, layers), mesh=mesh, in_specs=in_specs, out_specs=out_specs, check_vma=False
    )
```
